32 devices in a mesh: grp: 2 (over core), pen: 8 (over z, x), gz: 2 (over y).
Axes of the slice: x: 2, y: 2, z: 4, core: 2. Of those that a mesh axis runs over, the one named last changes fastest.
Arguments:
- velocity: float32 [4, 3, 4, 512, 256], P('grp', None, 'gz', 'pen'), may hold values from -6 to 6
- fringe_source: int32 [192], replicated, may hold values from 0 to 255
- blend_index: int32 [192], replicated, may hold values from 0 to 15
- blend_table: float32 [16], replicated, may hold values from 0.2 to 1
Outputs:
- velocity_next: float32 [4, 3, 4, 512, 256], P('grp', None, 'gz', 'pen')
The draws below stay inside these ranges and needn't reach their ends.
All inputs are finite; a program needn't handle non-finite values.
Results may differ from the reference program's by a relative error of at most 0.0003.
Values sent between devices are 32-bit elements; how exact they have to be, the bound alone decides.
A program may use at most 64 MiB of HBM per device.

```python
import jax
import jax.numpy as jnp
from jax import lax

NB = 256
NY = 512
NFR = 192
NTAB = 16
NZ = 4
SPAN_DEV = 64


def touch_ends(values, own_key, least, top_value):
    place = [jax.random.randint(jax.random.fold_in(own_key, axis), (), 0, length) for axis, length in enumerate(values.shape)]
    main_axis = values.shape.index(max(values.shape))
    next_to = place[:main_axis] + [(place[main_axis] + 1) % values.shape[main_axis]] + place[main_axis + 1:]
    return values.at[tuple(place)].set(least).at[tuple(next_to)].set(top_value)


def shard_levels(key, extent, shards, smallest, high):
    factor_of, own = 1.0, jax.random.fold_in(key, 6)
    for position, parts in shards:
        steps = jnp.exp(jax.random.uniform(jax.random.fold_in(own, position), (parts,), jnp.float32, smallest / len(shards), high / len(shards)))
        factor_of = factor_of * jnp.repeat(steps, extent[position] // parts).reshape([-1 if axis == position else 1 for axis in range(len(extent))])
    return factor_of


def bell_draw(key, shape, deviation, reach, split=(), held_as=jnp.bfloat16):
    entries = deviation * jax.random.normal(key, shape, jnp.float32)
    if split:
        entries = entries * shard_levels(key, shape, split, -0.22, 0.18)
    return jnp.clip(entries, -reach, reach).astype(held_as)


def setup_inputs(seed: int = 0) -> dict:
    keys = jax.random.split(jax.random.key(seed), 5)
    return {
        "velocity": bell_draw(keys[0], (4, 3, NZ, NY, NB), 1.0, 6.0, ((0, 2), (2, 2), (3, 8)), jnp.float32),
        "fringe_source": touch_ends(jax.random.randint(keys[1], (NFR,), 0, NB), jax.random.fold_in(keys[1], 1), 0, NB - 1).astype(jnp.int32),
        "blend_index": touch_ends(jax.random.randint(keys[2], (NFR,), 0, NTAB), jax.random.fold_in(keys[2], 1), 0, NTAB - 1).astype(jnp.int32),
        "blend_table": jnp.clip(jax.random.uniform(keys[3], (NTAB,), jnp.float32, 0.2, 1.0), 0.2, 1.0),
    }


SMAGORINSKY = 0.04
TIMESTEP = 0.1

def natural_order(field):
    lead_shape = field.shape[:-2]
    row_count = field.shape[-2]
    cell_count = field.shape[-1]
    groups = row_count // SPAN_DEV
    split_rows = field.reshape(lead_shape + (groups, SPAN_DEV, cell_count))
    return jnp.swapaxes(split_rows, -3, -2).reshape(field.shape)

def stored_order(field):
    lead_shape = field.shape[:-2]
    row_count = field.shape[-2]
    cell_count = field.shape[-1]
    groups = row_count // SPAN_DEV
    split_rows = field.reshape(lead_shape + (SPAN_DEV, groups, cell_count))
    return jnp.swapaxes(split_rows, -3, -2).reshape(field.shape)

def spectral_derivative(values, axis_index):
    length = values.shape[axis_index]
    coeffs = jnp.fft.rfft(values, axis=axis_index)
    mode_list = jnp.arange(length // 2 + 1)
    wavenum = jnp.where(mode_list == length // 2, 0.0, 2.0 * jnp.pi * mode_list / length)
    shape_list = [1] * values.ndim
    shape_list[axis_index] = length // 2 + 1
    factor = (1j * wavenum).reshape(shape_list)
    return jnp.fft.irfft(coeffs * factor, n=length, axis=axis_index).astype(values.dtype)

def strain_terms(col_speed, gradients):
    strain = {}
    squares = jnp.zeros_like(col_speed[0])
    for comp_a in range(3):
        for comp_b in range(comp_a, 3):
            strain_value = 0.5 * (gradients[comp_b][comp_a] + gradients[comp_a][comp_b])
            strain[comp_a, comp_b] = strain_value
            strain[comp_b, comp_a] = strain_value
            weight_sq = 1.0 if comp_a == comp_b else 2.0
            squares = squares + weight_sq * strain_value * strain_value
    eddy_visc = SMAGORINSKY * jnp.sqrt(2.0 * squares)
    fluxes = [jnp.stack([2.0 * eddy_visc * strain[comp_a, comp_b] for comp_a in range(3)]) for comp_b in range(3)]
    advect = sum((col_speed[comp_b][None] * gradients[comp_b] for comp_b in range(3)))
    return (fluxes, advect)

def domain_tendency(domain_field):
    levels = domain_field.shape[1]
    padded = jnp.pad(domain_field, ((0, 0), (2, 2), (0, 0), (0, 0)))

    def one_level(level_id):
        window = lax.dynamic_slice_in_dim(padded, level_id, 5, 1)
        centre = window[:, 1:4]
        gradients = (spectral_derivative(centre, -1), spectral_derivative(centre, -2), 0.5 * (window[:, 2:5] - window[:, 0:3]))
        fluxes, advect = strain_terms(centre, gradients)
        heights = level_id - 1 + jnp.arange(3, dtype=jnp.int32)
        inside = ((heights >= 0) & (heights < levels)).astype(domain_field.dtype)[None, :, None, None]
        flux_z = fluxes[2] * inside
        result = spectral_derivative(fluxes[0][:, 1], -1) + spectral_derivative(fluxes[1][:, 1], -2)
        result = result + 0.5 * (flux_z[:, 2] - flux_z[:, 0]) - advect[:, 1]
        return result
    stacked = lax.map(one_level, jnp.arange(levels, dtype=jnp.int32))
    return jnp.transpose(stacked, (1, 0, 2, 3))

def reference(velocity, fringe_source, blend_index, blend_table):
    blocks = [natural_order(velocity[block_id]) for block_id in range(4)]
    block_shape = blocks[0].shape
    farm_field = jnp.stack(blocks[:3], axis=-1).reshape(block_shape[:-1] + (3 * block_shape[-1],))
    inflow = blocks[3]
    farm_step = farm_field + TIMESTEP * domain_tendency(farm_field)
    inflow_step = inflow + TIMESTEP * domain_tendency(inflow)
    weights = blend_table[blend_index]
    source = jnp.take(inflow_step, fringe_source, axis=-1)
    fringe_head = farm_step[..., :NFR]
    blended = jnp.concatenate([fringe_head + weights * (source - fringe_head), farm_step[..., NFR:]], axis=-1)
    farm_blocks = blended.reshape(block_shape + (3,))
    return jnp.stack([stored_order(farm_blocks[..., 0]), stored_order(farm_blocks[..., 1]), stored_order(farm_blocks[..., 2]), stored_order(inflow_step)])
```

```python
import functools

import jax
import jax.numpy as jnp
import ml_dtypes
import numpy as np
from jax import lax
from jax.experimental import pallas as pl
from jax.experimental.pallas import tpu as pltpu
from jax.sharding import PartitionSpec as P

SMAGORINSKY = 0.04
TIMESTEP = 0.1
LANES = 128
SLAB = 16
MESH = pl.DeviceIdType.MESH
F32 = jnp.float32
BF16 = jnp.bfloat16


def cotangent_entries(offset, length):
    half = length // 2
    reduced = (offset + half) % length - half
    angle = np.pi * reduced / length
    safe = np.where(reduced != 0, np.sin(angle), 1.0)
    sign = 1.0 - 2.0 * (reduced % 2)
    return np.where(reduced != 0, sign * (np.pi / length) * np.cos(angle) / safe, 0.0)


def span_table(line_length, groups):
    rows_each = line_length // groups
    order = np.arange(line_length)
    cell = order % rows_each * groups + order // rows_each
    return cotangent_entries(cell[:, None] - cell[None, :], line_length)


def stream_table(width):
    cells = np.arange(width)
    tables = []
    for group in range(2):
        outs = (2 * group, 2 * group + 1)
        ins = outs + (2 - 2 * group, 3 - 2 * group)
        rows = []
        for i in ins:
            row = []
            for o in outs:
                if i < 3 and o < 3:
                    offset = (o + 3 * cells)[None, :] - (i + 3 * cells)[:, None]
                    row.append(cotangent_entries(offset, 3 * width))
                elif i == o:
                    row.append(cotangent_entries(cells[None, :] - cells[:, None], width))
                else:
                    row.append(np.zeros((width, width)))
            rows.append(np.concatenate(row, axis=1))
        tables.append(np.concatenate(rows, axis=0))
    return np.stack(tables)


def two_parts(table):
    high = table.astype(np.float32).astype(ml_dtypes.bfloat16)
    low = (table - high.astype(np.float64)).astype(np.float32).astype(ml_dtypes.bfloat16)
    return np.stack([high, low])


def split(x):
    high = x.astype(BF16)
    return high, (x - high.astype(F32)).astype(BF16)


def dot(a, b):
    return jnp.dot(a, b, preferred_element_type=F32)


def kernel(
    pens, heights, u, source, index, table, wx_hbm, wy_hbm, out,
    wx, wy, upad, urecv, gx, gy, fx, fy, fz, frecv, acc, dy, colu, coly, colf, cold,
    hi, lo, inflow, send, recv, esend, erecv, hsend, hrecv, isend, irecv, lsem,
):
    g = lax.axis_index("grp")
    me = lax.axis_index("pen")
    s = lax.axis_index("gz")
    _, _, levels, rows, width = u.shape
    halves = width // LANES
    chunks = 2 * 3 * levels * halves // pens
    group_count = 2 * levels * halves
    other = 1 - g
    below, above = s > 0, s < heights - 1

    wx_copy = pltpu.make_async_copy(wx_hbm.at[:, g], wx, lsem.at[0])
    wy_copy = pltpu.make_async_copy(wy_hbm, wy, lsem.at[1])
    u_copy = pltpu.make_async_copy(u, upad.at[:, :, pl.ds(1, levels)], lsem.at[2])
    wy_copy.start()
    wx_copy.start()
    u_copy.start()

    barrier = pltpu.get_barrier_semaphore()

    @pl.loop(1, pens)
    def _(i):
        pl.semaphore_signal(
            barrier, inc=1, device_id={"pen": lax.rem(me + i, pens)}, device_id_type=MESH
        )

    pl.semaphore_signal(barrier, inc=1, device_id={"grp": other}, device_id_type=MESH)

    @pl.when(below)
    def _():
        pl.semaphore_signal(barrier, inc=1, device_id={"gz": s - 1}, device_id_type=MESH)

    @pl.when(above)
    def _():
        pl.semaphore_signal(barrier, inc=1, device_id={"gz": s + 1}, device_id_type=MESH)

    levels_near = below.astype(jnp.int32) + above.astype(jnp.int32)
    pl.semaphore_wait(barrier, pens + levels_near)

    def place(group):
        b = 1 - lax.div(group, levels * halves)
        z = lax.rem(lax.div(group, halves), levels)
        return b, z, pl.ds(pl.multiple_of(lax.rem(group, halves) * LANES, LANES), LANES)

    def unit(k, q):
        t = k * pens + q
        b, z, x = place(lax.div(t, 3))
        return b, lax.rem(t, 3), z, slice(None), x

    def band(q):
        return pl.ds(pl.multiple_of(q * rows, rows), rows)

    def pen_copy(src, dst, phase, k, i, q):
        return pltpu.make_async_remote_copy(
            src_ref=src, dst_ref=dst, send_sem=send.at[phase, k, i],
            recv_sem=recv.at[phase, k, i], device_id={"pen": q}, device_id_type=MESH,
        )

    def own_copy(src, dst, phase, k):
        return pltpu.make_async_copy(src, dst, send.at[phase, k, 0])

    def to_lines(field, lines, phase, k):
        own_copy(field.at[unit(k, me)], lines.at[k, band(me)], phase, k).start()

        @pl.loop(1, pens)
        def _(i):
            q = lax.rem(me + i, pens)
            pen_copy(field.at[unit(k, q)], lines.at[k, band(me)], phase, k, i, q).start()

    def lines_here(field, lines, phase, k):
        own_copy(field.at[unit(k, me)], lines.at[k, band(me)], phase, k).wait()

        @pl.loop(1, pens)
        def _(i):
            q = lax.rem(me + pens - i, pens)
            pen_copy(field.at[unit(k, q)], lines.at[k, band(q)], phase, k, i, q).wait_recv()

    def to_rows(lines, field, phase, k):
        own_copy(lines.at[k, band(me)], field.at[unit(k, me)], phase, k).start()

        @pl.loop(1, pens)
        def _(i):
            q = lax.rem(me + i, pens)
            pen_copy(lines.at[k, band(q)], field.at[unit(k, me)], phase, k, i, q).start()

    def rows_here(lines, field, phase, k):
        own_copy(lines.at[k, band(me)], field.at[unit(k, me)], phase, k).wait()

        @pl.loop(1, pens)
        def _(i):
            q = lax.rem(me + pens - i, pens)
            pen_copy(lines.at[k, band(q)], field.at[unit(k, q)], phase, k, i, q).wait_recv()

    def sent(src, dst, phase):
        for k in range(chunks):

            @pl.loop(1, pens)
            def _(i, k=k):
                pen_copy(src, dst, phase, k, i, lax.rem(me + i, pens)).wait_send()

    def span(lines, result, k):
        high, low = split(lines[k])
        both = dot(wy[0], jnp.concatenate([high, low], axis=1))
        result[k] = both[:, :LANES] + both[:, LANES:] + dot(wy[1], high)

    def exchange(src, dst, n):
        return pltpu.make_async_remote_copy(
            src_ref=src, dst_ref=dst, send_sem=esend.at[n], recv_sem=erecv.at[n],
            device_id={"grp": other}, device_id_type=MESH,
        )

    def stream(mine, theirs):
        for b in range(2):
            for at, field in ((b, mine), (b + 2, theirs)):
                high, low = split(field[b].reshape(3 * levels * rows, width))
                hi[:, at * width : (at + 1) * width] = high
                lo[:, at * width : (at + 1) * width] = low

    def stream_out(b):
        cols = slice(b * width, (b + 1) * width)
        part = dot(hi[...], wx[0, :, cols]) + dot(hi[...], wx[1, :, cols])
        part = part + dot(lo[...], wx[0, :, cols])
        return part.reshape(3, levels, rows, width)

    def up_copy(field, n):
        return pltpu.make_async_remote_copy(
            src_ref=field.at[:, :, levels], dst_ref=field.at[:, :, 0],
            send_sem=hsend.at[n, 0], recv_sem=hrecv.at[n, 0],
            device_id={"gz": s + 1}, device_id_type=MESH,
        )

    def down_copy(field, n):
        return pltpu.make_async_remote_copy(
            src_ref=field.at[:, :, 1], dst_ref=field.at[:, :, levels + 1],
            send_sem=hsend.at[n, 1], recv_sem=hrecv.at[n, 1],
            device_id={"gz": s - 1}, device_id_type=MESH,
        )

    def send_levels(field, n):
        @pl.when(above)
        def _():
            up_copy(field, n).start()

        @pl.when(below)
        def _():
            down_copy(field, n).start()

    def levels_here(field, n):
        edge = jnp.zeros((2, 3, rows, width), F32)

        @pl.when(below)
        def _():
            down_copy(field, n).wait_send()
            up_copy(field, n).wait_recv()

        @pl.when(jnp.logical_not(below))
        def _():
            field[:, :, 0] = edge

        @pl.when(above)
        def _():
            up_copy(field, n).wait_send()
            down_copy(field, n).wait_recv()

        @pl.when(jnp.logical_not(above))
        def _():
            field[:, :, levels + 1] = edge

    def over_slabs(first, last, step):
        @pl.loop(first * (rows // SLAB), last * (rows // SLAB))
        def _(n):
            b, z, x = place(lax.div(n, rows // SLAB))
            r = pl.ds(pl.multiple_of(lax.rem(n, rows // SLAB) * SLAB, SLAB), SLAB)
            step(b, z, r, x)

    def fluxes(b, z, r, x):
        speed = [u[b, c, z, r, x] for c in range(3)]
        grad = [
            [gx[b, c, z, r, x] for c in range(3)],
            [gy[b, c, z, r, x] for c in range(3)],
            [0.5 * (upad[b, c, z + 2, r, x] - upad[b, c, z, r, x]) for c in range(3)],
        ]
        for c in range(3):
            acc[b, c, z, r, x] = -(
                speed[0] * grad[0][c] + speed[1] * grad[1][c] + speed[2] * grad[2][c]
            )
        strain = {}
        squares = 0.0
        for i in range(3):
            for j in range(i, 3):
                value = grad[i][i] if i == j else 0.5 * (grad[i][j] + grad[j][i])
                strain[i, j] = strain[j, i] = value
                squares = squares + (1.0 if i == j else 2.0) * value * value
        eddy = (2.0 * SMAGORINSKY) * jnp.sqrt(2.0 * squares)
        for c in range(3):
            fx[b, c, z, r, x] = eddy * strain[c, 0]
            fy[b, c, z, r, x] = eddy * strain[c, 1]
            fz[b, c, z + 1, r, x] = eddy * strain[c, 2]

    def add_rest(b, z, r, x):
        for c in range(3):
            rise = 0.5 * (fz[b, c, z + 2, r, x] - fz[b, c, z, r, x])
            total = acc[b, c, z, r, x] + gx[b, c, z, r, x] + rise
            acc[b, c, z, r, x] = u[b, c, z, r, x] + TIMESTEP * total

    def add_span(b, z, r, x):
        for c in range(3):
            out[b, c, z, r, x] = acc[b, c, z, r, x] + TIMESTEP * dy[b, c, z, r, x]

    def groups_ready(k):
        return (k + 1) * pens // 3

    def groups_needed(k):
        return -(-((k + 1) * pens) // 3)

    x_exchange = exchange(u, urecv, 0)
    x_exchange.start()
    u_copy.wait()
    for k in range(chunks):
        to_lines(u, colu, 0, k)
        if k == 0:
            send_levels(upad, 0)
    wy_copy.wait()
    lines_here(u, colu, 0, 0)
    span(colu, coly, 0)
    to_rows(coly, gy, 1, 0)
    wx_copy.wait()
    x_exchange.wait()
    stream(u, urecv)
    for b in range(2):
        gx[b] = stream_out(b)
    for k in range(1, chunks):
        lines_here(u, colu, 0, k)
        span(colu, coly, k)
        to_rows(coly, gy, 1, k)
    levels_here(upad, 0)

    done, started = 0, 0
    for k in range(chunks):
        rows_here(coly, gy, 1, k)
        over_slabs(done, groups_ready(k), fluxes)
        done = groups_ready(k)
        while started < chunks and groups_needed(started) <= done:
            to_lines(fy, colf, 2, started)
            started += 1

    flux_exchange = exchange(fx, frecv, 1)
    flux_exchange.start()
    send_levels(fz, 1)

    columns = index.shape[1]
    third = columns // 3
    weight = jnp.zeros((1, columns), F32)
    for t in range(table.shape[0]):
        weight = weight + jnp.where(index[...] == t, table[t], 0.0)
    weight = jnp.broadcast_to(weight, (8, columns))
    cell = lax.broadcasted_iota(jnp.int32, (width, columns), 0)
    chosen = jnp.where(cell == source[...], 1.0, 0.0).astype(BF16)
    plane = lax.broadcasted_iota(jnp.int32, (columns, LANES), 0)
    slot = lax.broadcasted_iota(jnp.int32, (columns, LANES), 1)
    picks, weights = [], []
    for b in range(2):
        first = 2 * g if b == 0 else 1 - 4 * columns * g
        spread = jnp.where(
            jnp.logical_and(plane == 3 * slot + first, slot < third), 1.0, 0.0
        )
        picks.append(dot(chosen, spread.astype(BF16)).astype(BF16))
        weights.append(
            jnp.dot(weight, spread, precision=lax.Precision.HIGHEST, preferred_element_type=F32)
        )

    lines_here(fy, colf, 2, 0)
    span(colf, cold, 0)
    to_rows(cold, dy, 3, 0)
    flux_exchange.wait()
    stream(fx, frecv)
    for b in range(2):
        gx[b] = stream_out(b)
    for k in range(1, chunks):
        lines_here(fy, colf, 2, k)
        span(colf, cold, k)
        to_rows(cold, dy, 3, k)
    levels_here(fz, 1)
    over_slabs(0, group_count, add_rest)

    def blend(b, feed):
        high, low = feed
        fed = (dot(high, picks[b]) + dot(low, picks[b])).reshape(3, levels, rows, LANES)
        head = out[b, :, :, :, :LANES]
        out[b, :, :, :, :LANES] = head + weights[b][0:1] * (fed - head)

    inflow_copy = pltpu.make_async_remote_copy(
        src_ref=out.at[1], dst_ref=inflow, send_sem=isend, recv_sem=irecv,
        device_id={"grp": other}, device_id_type=MESH,
    )
    done = 0
    for k in range(chunks):
        rows_here(cold, dy, 3, k)
        ready = groups_ready(k)
        half = group_count // 2
        if done < half <= ready:
            over_slabs(done, half, add_span)
            done = half

            @pl.when(g == 1)
            def _():
                inflow_copy.start()
                inflow[...] = out[1]

        over_slabs(done, ready, add_span)
        done = ready

    @pl.when(g == 0)
    def _():
        inflow_copy.wait_recv()

    @pl.when(g == 1)
    def _():
        inflow_copy.wait_send()

    feed = split(inflow[...].reshape(3 * levels * rows, width))
    for b in range(2):
        blend(b, feed)
    for phase, src, dst in (
        (0, u.at[unit(0, 0)], colu.at[0, band(0)]),
        (1, coly.at[0, band(0)], gy.at[unit(0, 0)]),
        (2, fy.at[unit(0, 0)], colf.at[0, band(0)]),
        (3, cold.at[0, band(0)], dy.at[unit(0, 0)]),
    ):
        sent(src, dst, phase)


def per_device(pens, heights, velocity, source, index, table):
    _, _, levels, rows, width = velocity.shape
    line = rows * pens
    chunks = 2 * 3 * levels * (width // LANES) // pens
    wx = two_parts(stream_table(width))
    wy = two_parts(span_table(line, pens))
    flat = 3 * levels * rows
    whole = pltpu.VMEM(velocity.shape, F32)
    padded = pltpu.VMEM((2, 3, levels + 2, rows, width), F32)
    lines = pltpu.VMEM((chunks, line, LANES), F32)
    vmem = pl.BlockSpec(memory_space=pltpu.VMEM)
    dma = pltpu.SemaphoreType.DMA
    return pl.pallas_call(
        functools.partial(kernel, pens, heights),
        out_shape=jax.ShapeDtypeStruct(velocity.shape, F32),
        in_specs=[
            vmem, vmem, vmem, pl.BlockSpec(memory_space=pltpu.SMEM),
            pl.BlockSpec(memory_space=pl.ANY), pl.BlockSpec(memory_space=pl.ANY),
        ],
        out_specs=vmem,
        scratch_shapes=[
            pltpu.VMEM((2, 4 * width, 2 * width), BF16),
            pltpu.VMEM((2, line, line), BF16),
            padded, whole, whole, whole, whole, whole, padded, whole, whole, whole,
            lines, lines, lines, lines,
            pltpu.VMEM((flat, 4 * width), BF16),
            pltpu.VMEM((flat, 4 * width), BF16),
            pltpu.VMEM(velocity.shape[1:], F32),
            dma((4, chunks, pens)), dma((4, chunks, pens)),
            dma((2,)), dma((2,)), dma((2, 2)), dma((2, 2)), dma, dma, dma((3,)),
        ],
        compiler_params=pltpu.CompilerParams(
            collective_id=0, has_side_effects=True, vmem_limit_bytes=56 * 1024 * 1024
        ),
    )(velocity, source.reshape(1, -1), index.reshape(1, -1), table, jnp.asarray(wx), jnp.asarray(wy))


def solution(mesh):
    placed = P("grp", None, "gz", "pen", None)
    return jax.shard_map(
        functools.partial(per_device, mesh.shape["pen"], mesh.shape["gz"]),
        mesh=mesh,
        in_specs=(placed, P(), P(), P()),
        out_specs=placed,
        check_vma=False,
    )
```

```python
import functools

import jax
import jax.numpy as jnp
import ml_dtypes
import numpy as np
from jax import lax
from jax.experimental import pallas as pl
from jax.experimental.pallas import tpu as pltpu
from jax.sharding import PartitionSpec as P

SMAGORINSKY = 0.04
TIMESTEP = 0.1
LANES = 128
SLAB = 16
MESH = pl.DeviceIdType.MESH
F32 = jnp.float32
BF16 = jnp.bfloat16


def cotangent_entries(offset, length):
    half = length // 2
    reduced = (offset + half) % length - half
    angle = np.pi * reduced / length
    safe = np.where(reduced != 0, np.sin(angle), 1.0)
    sign = 1.0 - 2.0 * (reduced % 2)
    return np.where(reduced != 0, sign * (np.pi / length) * np.cos(angle) / safe, 0.0)


def span_table(line_length, groups):
    rows_each = line_length // groups
    order = np.arange(line_length)
    cell = order % rows_each * groups + order // rows_each
    return cotangent_entries(cell[:, None] - cell[None, :], line_length)


def stream_table(width):
    cells = np.arange(width)
    tables = []
    for group in range(2):
        outs = (2 * group, 2 * group + 1)
        ins = outs + (2 - 2 * group, 3 - 2 * group)
        rows = []
        for i in ins:
            row = []
            for o in outs:
                if i < 3 and o < 3:
                    offset = (o + 3 * cells)[None, :] - (i + 3 * cells)[:, None]
                    row.append(cotangent_entries(offset, 3 * width))
                elif i == o:
                    row.append(cotangent_entries(cells[None, :] - cells[:, None], width))
                else:
                    row.append(np.zeros((width, width)))
            rows.append(np.concatenate(row, axis=1))
        tables.append(np.concatenate(rows, axis=0))
    return np.stack(tables)


def two_parts(table):
    high = table.astype(np.float32).astype(ml_dtypes.bfloat16)
    low = (table - high.astype(np.float64)).astype(np.float32).astype(ml_dtypes.bfloat16)
    return np.stack([high, low])


def split(x):
    high = x.astype(BF16)
    return high, (x - high.astype(F32)).astype(BF16)


def dot(a, b):
    return jnp.dot(a, b, preferred_element_type=F32)


def kernel(
    pens, heights, u, source, index, table, wx_hbm, wy_hbm, out,
    wx, wy, upad, urecv, gx, gy, fx, fy, fz, frecv, acc, dy, colu, coly, colf, cold,
    hi, lo, inflow, fed, send, recv, esend, erecv, hsend, hrecv, isend, irecv, lsem,
):
    g = lax.axis_index("grp")
    me = lax.axis_index("pen")
    s = lax.axis_index("gz")
    _, _, levels, rows, width = u.shape
    halves = width // LANES
    chunks = 2 * 3 * levels * halves // pens
    group_count = 2 * levels * halves
    other = 1 - g
    below, above = s > 0, s < heights - 1

    barrier = pltpu.get_barrier_semaphore()

    @pl.loop(1, pens)
    def _(i):
        pl.semaphore_signal(
            barrier, inc=1, device_id={"pen": lax.rem(me + i, pens)}, device_id_type=MESH
        )

    pl.semaphore_signal(barrier, inc=1, device_id={"grp": other}, device_id_type=MESH)

    @pl.when(below)
    def _():
        pl.semaphore_signal(barrier, inc=1, device_id={"gz": s - 1}, device_id_type=MESH)

    @pl.when(above)
    def _():
        pl.semaphore_signal(barrier, inc=1, device_id={"gz": s + 1}, device_id_type=MESH)

    wx_copy = pltpu.make_async_copy(wx_hbm.at[:, g], wx, lsem.at[0])
    wy_copy = pltpu.make_async_copy(wy_hbm, wy, lsem.at[1])
    u_copy = pltpu.make_async_copy(u, upad.at[:, :, pl.ds(1, levels)], lsem.at[2])
    u_copy.start()
    wy_copy.start()
    wx_copy.start()

    levels_near = below.astype(jnp.int32) + above.astype(jnp.int32)
    pl.semaphore_wait(barrier, pens + levels_near)

    def place(group):
        b = 1 - lax.div(group, levels * halves)
        z = lax.rem(lax.div(group, halves), levels)
        return b, z, pl.ds(pl.multiple_of(lax.rem(group, halves) * LANES, LANES), LANES)

    def unit(k, q):
        t = k * pens + q
        b, z, x = place(lax.div(t, 3))
        return b, lax.rem(t, 3), z, slice(None), x

    def band(q):
        return pl.ds(pl.multiple_of(q * rows, rows), rows)

    def pen_copy(src, dst, phase, k, i, q):
        return pltpu.make_async_remote_copy(
            src_ref=src, dst_ref=dst, send_sem=send.at[phase, k, i],
            recv_sem=recv.at[phase, k, i], device_id={"pen": q}, device_id_type=MESH,
        )

    def own_copy(src, dst, phase, k):
        return pltpu.make_async_copy(src, dst, send.at[phase, k, 0])

    def to_lines(field, lines, phase, k):
        own_copy(field.at[unit(k, me)], lines.at[k, band(me)], phase, k).start()

        @pl.loop(1, pens)
        def _(i):
            q = lax.rem(me + i, pens)
            pen_copy(field.at[unit(k, q)], lines.at[k, band(me)], phase, k, i, q).start()

    def lines_here(field, lines, phase, k):
        own_copy(field.at[unit(k, me)], lines.at[k, band(me)], phase, k).wait()

        @pl.loop(1, pens)
        def _(i):
            q = lax.rem(me + pens - i, pens)
            pen_copy(field.at[unit(k, q)], lines.at[k, band(q)], phase, k, i, q).wait_recv()

    def to_rows(lines, field, phase, k):
        own_copy(lines.at[k, band(me)], field.at[unit(k, me)], phase, k).start()

        @pl.loop(1, pens)
        def _(i):
            q = lax.rem(me + i, pens)
            pen_copy(lines.at[k, band(q)], field.at[unit(k, me)], phase, k, i, q).start()

    def rows_here(lines, field, phase, k):
        own_copy(lines.at[k, band(me)], field.at[unit(k, me)], phase, k).wait()

        @pl.loop(1, pens)
        def _(i):
            q = lax.rem(me + pens - i, pens)
            pen_copy(lines.at[k, band(q)], field.at[unit(k, q)], phase, k, i, q).wait_recv()

    def sent(src, dst, phase):
        for k in range(chunks):

            @pl.loop(1, pens)
            def _(i, k=k):
                pen_copy(src, dst, phase, k, i, lax.rem(me + i, pens)).wait_send()

    def span(lines, result, k):
        high, low = split(lines[k])
        both = dot(wy[0], jnp.concatenate([high, low], axis=1))
        result[k] = both[:, :LANES] + both[:, LANES:] + dot(wy[1], high)

    def exchange(src, dst, n):
        return pltpu.make_async_remote_copy(
            src_ref=src, dst_ref=dst, send_sem=esend.at[n], recv_sem=erecv.at[n],
            device_id={"grp": other}, device_id_type=MESH,
        )

    def stream(mine, theirs):
        for b in range(2):
            for at, field in ((b, mine(b)), (b + 2, theirs[b])):
                high, low = split(field.reshape(3 * levels * rows, width))
                hi[:, at * width : (at + 1) * width] = high
                lo[:, at * width : (at + 1) * width] = low

    def stream_out(b):
        cols = slice(b * width, (b + 1) * width)
        part = dot(hi[...], wx[0, :, cols]) + dot(hi[...], wx[1, :, cols])
        part = part + dot(lo[...], wx[0, :, cols])
        return part.reshape(3, levels, rows, width)

    def up_copy(field, n):
        return pltpu.make_async_remote_copy(
            src_ref=field.at[:, :, levels], dst_ref=field.at[:, :, 0],
            send_sem=hsend.at[n, 0], recv_sem=hrecv.at[n, 0],
            device_id={"gz": s + 1}, device_id_type=MESH,
        )

    def down_copy(field, n):
        return pltpu.make_async_remote_copy(
            src_ref=field.at[:, :, 1], dst_ref=field.at[:, :, levels + 1],
            send_sem=hsend.at[n, 1], recv_sem=hrecv.at[n, 1],
            device_id={"gz": s - 1}, device_id_type=MESH,
        )

    def send_levels(field, n):
        @pl.when(above)
        def _():
            up_copy(field, n).start()

        @pl.when(below)
        def _():
            down_copy(field, n).start()

    def levels_here(field, n):
        edge = jnp.zeros((2, 3, rows, width), F32)

        @pl.when(below)
        def _():
            down_copy(field, n).wait_send()
            up_copy(field, n).wait_recv()

        @pl.when(jnp.logical_not(below))
        def _():
            field[:, :, 0] = edge

        @pl.when(above)
        def _():
            up_copy(field, n).wait_send()
            down_copy(field, n).wait_recv()

        @pl.when(jnp.logical_not(above))
        def _():
            field[:, :, levels + 1] = edge

    def over_slabs(first, last, step):
        @pl.loop(first * (rows // SLAB), last * (rows // SLAB))
        def _(n):
            b, z, x = place(lax.div(n, rows // SLAB))
            r = pl.ds(pl.multiple_of(lax.rem(n, rows // SLAB) * SLAB, SLAB), SLAB)
            step(b, z, r, x)

    def fluxes(b, z, r, x):
        speed = [upad[b, c, z + 1, r, x] for c in range(3)]
        grad = [
            [gx[b, c, z, r, x] for c in range(3)],
            [gy[b, c, z, r, x] for c in range(3)],
            [0.5 * (upad[b, c, z + 2, r, x] - upad[b, c, z, r, x]) for c in range(3)],
        ]
        for c in range(3):
            acc[b, c, z, r, x] = -(
                speed[0] * grad[0][c] + speed[1] * grad[1][c] + speed[2] * grad[2][c]
            )
        strain = {}
        squares = 0.0
        for i in range(3):
            for j in range(i, 3):
                value = grad[i][i] if i == j else 0.5 * (grad[i][j] + grad[j][i])
                strain[i, j] = strain[j, i] = value
                squares = squares + (1.0 if i == j else 2.0) * value * value
        eddy = (2.0 * SMAGORINSKY) * jnp.sqrt(2.0 * squares)
        for c in range(3):
            fx[b, c, z, r, x] = eddy * strain[c, 0]
            fy[b, c, z, r, x] = eddy * strain[c, 1]
            fz[b, c, z + 1, r, x] = eddy * strain[c, 2]

    def add_rest(b, z, r, x):
        for c in range(3):
            rise = 0.5 * (fz[b, c, z + 2, r, x] - fz[b, c, z, r, x])
            total = acc[b, c, z, r, x] + gx[b, c, z, r, x] + rise
            acc[b, c, z, r, x] = upad[b, c, z + 1, r, x] + TIMESTEP * total

    def add_span(b, z, r, x):
        for c in range(3):
            out[b, c, z, r, x] = acc[b, c, z, r, x] + TIMESTEP * dy[b, c, z, r, x]

    def groups_ready(k):
        return (k + 1) * pens // 3

    def groups_needed(k):
        return -(-((k + 1) * pens) // 3)

    x_exchange = exchange(u, urecv, 0)
    for k in range(min(2, chunks)):
        to_lines(u, colu, 0, k)
        if k == 0:
            x_exchange.start()
    u_copy.wait()
    send_levels(upad, 0)
    wy_copy.wait()
    lines_here(u, colu, 0, 0)
    span(colu, coly, 0)
    to_rows(coly, gy, 1, 0)
    for k in range(2, chunks):
        to_lines(u, colu, 0, k)
    wx_copy.wait()
    x_exchange.wait()
    stream(lambda b: upad[b, :, 1 : levels + 1], urecv)
    for b in range(2):
        gx[b] = stream_out(b)
    for k in range(1, chunks):
        lines_here(u, colu, 0, k)
        span(colu, coly, k)
        to_rows(coly, gy, 1, k)
    levels_here(upad, 0)

    done, started = 0, 0
    for k in range(chunks):
        rows_here(coly, gy, 1, k)
        over_slabs(done, groups_ready(k), fluxes)
        done = groups_ready(k)
        while started < chunks and groups_needed(started) <= done:
            to_lines(fy, colf, 2, started)
            started += 1

    flux_exchange = exchange(fx, frecv, 1)
    flux_exchange.start()
    send_levels(fz, 1)

    columns = index.shape[1]
    third = columns // 3
    weight = jnp.zeros((1, columns), F32)
    for t in range(table.shape[0]):
        weight = weight + jnp.where(index[...] == t, table[t], 0.0)
    weight = jnp.broadcast_to(weight, (8, columns))
    cell = lax.broadcasted_iota(jnp.int32, (width, columns), 0)
    chosen = jnp.where(cell == source[...], 1.0, 0.0).astype(BF16)
    plane = lax.broadcasted_iota(jnp.int32, (columns, LANES), 0)
    slot = lax.broadcasted_iota(jnp.int32, (columns, LANES), 1)
    picks, weights = [], []
    for b in range(2):
        first = 2 * g if b == 0 else 1 - 4 * columns * g
        spread = jnp.where(
            jnp.logical_and(plane == 3 * slot + first, slot < third), 1.0, 0.0
        )
        picks.append(dot(chosen, spread.astype(BF16)).astype(BF16))
        weights.append(
            jnp.dot(weight, spread, precision=lax.Precision.HIGHEST, preferred_element_type=F32)
        )

    lines_here(fy, colf, 2, 0)
    span(colf, cold, 0)
    to_rows(cold, dy, 3, 0)
    flux_exchange.wait()
    stream(lambda b: fx[b], frecv)
    for b in range(2):
        gx[b] = stream_out(b)
    for k in range(1, chunks):
        lines_here(fy, colf, 2, k)
        span(colf, cold, k)
        to_rows(cold, dy, 3, k)
    levels_here(fz, 1)
    over_slabs(0, group_count, add_rest)

    def feed(b, parts):
        both = dot(parts[0], picks[b]) + dot(parts[1], picks[b])
        fed[b] = both.reshape(3, levels, rows, LANES)

    def blend(b, z):
        head = out[b, :, z, :, :LANES]
        out[b, :, z, :, :LANES] = head + weights[b][0:1] * (fed[b, :, z] - head)

    inflow_copy = pltpu.make_async_remote_copy(
        src_ref=out.at[1], dst_ref=inflow, send_sem=isend, recv_sem=irecv,
        device_id={"grp": other}, device_id_type=MESH,
    )
    done, half = 0, group_count // 2
    for k in range(chunks):
        rows_here(cold, dy, 3, k)
        ready = groups_ready(k)
        if done < half <= ready:
            over_slabs(done, half, add_span)
            done = half

            @pl.when(g == 1)
            def _():
                inflow_copy.start()
                inflow[...] = out[1]

            over_slabs(done, ready, add_span)
            done = ready

            @pl.when(g == 0)
            def _():
                inflow_copy.wait_recv()

            @pl.when(g == 1)
            def _():
                inflow_copy.wait_send()

            parts = split(inflow[...].reshape(3 * levels * rows, width))
            for b in range(2):
                feed(b, parts)
            for z in range(levels):
                blend(1, z)
        elif done < ready:
            over_slabs(done, ready, add_span)
            done = ready
    for z in range(levels):
        blend(0, z)
    for phase, src, dst in (
        (0, u.at[unit(0, 0)], colu.at[0, band(0)]),
        (1, coly.at[0, band(0)], gy.at[unit(0, 0)]),
        (2, fy.at[unit(0, 0)], colf.at[0, band(0)]),
        (3, cold.at[0, band(0)], dy.at[unit(0, 0)]),
    ):
        sent(src, dst, phase)


def per_device(pens, heights, velocity, source, index, table):
    _, _, levels, rows, width = velocity.shape
    line = rows * pens
    chunks = 2 * 3 * levels * (width // LANES) // pens
    wx = two_parts(stream_table(width))
    wy = two_parts(span_table(line, pens))
    flat = 3 * levels * rows
    whole = pltpu.VMEM(velocity.shape, F32)
    padded = pltpu.VMEM((2, 3, levels + 2, rows, width), F32)
    lines = pltpu.VMEM((chunks, line, LANES), F32)
    vmem = pl.BlockSpec(memory_space=pltpu.VMEM)
    dma = pltpu.SemaphoreType.DMA
    return pl.pallas_call(
        functools.partial(kernel, pens, heights),
        out_shape=pltpu.VMEM(velocity.shape, F32),
        in_specs=[
            pl.BlockSpec(memory_space=pl.ANY), vmem, vmem, pl.BlockSpec(memory_space=pltpu.SMEM),
            pl.BlockSpec(memory_space=pl.ANY), pl.BlockSpec(memory_space=pl.ANY),
        ],
        out_specs=vmem,
        scratch_shapes=[
            pltpu.VMEM((2, 4 * width, 2 * width), BF16),
            pltpu.VMEM((2, line, line), BF16),
            padded, whole, whole, whole, whole, whole, padded, whole, whole, whole,
            lines, lines, lines, lines,
            pltpu.VMEM((flat, 4 * width), BF16),
            pltpu.VMEM((flat, 4 * width), BF16),
            pltpu.VMEM(velocity.shape[1:], F32),
            pltpu.VMEM((2, 3, levels, rows, LANES), F32),
            dma((4, chunks, pens)), dma((4, chunks, pens)),
            dma((2,)), dma((2,)), dma((2, 2)), dma((2, 2)), dma, dma, dma((3,)),
        ],
        compiler_params=pltpu.CompilerParams(
            collective_id=0, has_side_effects=True, vmem_limit_bytes=56 * 1024 * 1024
        ),
    )(velocity, source.reshape(1, -1), index.reshape(1, -1), table, jnp.asarray(wx), jnp.asarray(wy))


def solution(mesh):
    placed = P("grp", None, "gz", "pen", None)
    return jax.shard_map(
        functools.partial(per_device, mesh.shape["pen"], mesh.shape["gz"]),
        mesh=mesh,
        in_specs=(placed, P(), P(), P()),
        out_specs=placed,
        check_vma=False,
    )
```

```python
import functools

import jax
import jax.numpy as jnp
import ml_dtypes
import numpy as np
from jax import lax
from jax.experimental import pallas as pl
from jax.experimental.pallas import tpu as pltpu
from jax.sharding import PartitionSpec as P

SMAGORINSKY = 0.04
TIMESTEP = 0.1
LANES = 128
SLAB = 16
MESH = pl.DeviceIdType.MESH
F32 = jnp.float32
BF16 = jnp.bfloat16


def cotangent_entries(offset, length):
    half = length // 2
    reduced = (offset + half) % length - half
    angle = np.pi * reduced / length
    safe = np.where(reduced != 0, np.sin(angle), 1.0)
    sign = 1.0 - 2.0 * (reduced % 2)
    return np.where(reduced != 0, sign * (np.pi / length) * np.cos(angle) / safe, 0.0)


def span_table(line_length, groups):
    rows_each = line_length // groups
    order = np.arange(line_length)
    cell = order % rows_each * groups + order // rows_each
    return cotangent_entries(cell[:, None] - cell[None, :], line_length)


def stream_table(width):
    cells = np.arange(width)
    tables = []
    for group in range(2):
        outs = (2 * group, 2 * group + 1)
        ins = outs + (2 - 2 * group, 3 - 2 * group)
        rows = []
        for i in ins:
            row = []
            for o in outs:
                if i < 3 and o < 3:
                    offset = (o + 3 * cells)[None, :] - (i + 3 * cells)[:, None]
                    row.append(cotangent_entries(offset, 3 * width))
                elif i == o:
                    row.append(cotangent_entries(cells[None, :] - cells[:, None], width))
                else:
                    row.append(np.zeros((width, width)))
            rows.append(np.concatenate(row, axis=1))
        tables.append(np.concatenate(rows, axis=0))
    return np.stack(tables)


def two_parts(table):
    high = table.astype(np.float32).astype(ml_dtypes.bfloat16)
    low = (table - high.astype(np.float64)).astype(np.float32).astype(ml_dtypes.bfloat16)
    return np.stack([high, low])


def split(x):
    high = x.astype(BF16)
    return high, (x - high.astype(F32)).astype(BF16)


def dot(a, b):
    return jnp.dot(a, b, preferred_element_type=F32)


def kernel(
    pens, heights, u, source, index, table, wx_hbm, wy_hbm, out,
    wx, wy, upad, urecv, gx, gy, fx, fy, fz, frecv, acc, dy, colu, coly, colf, cold,
    hi, lo, inflow, fed, send, recv, esend, erecv, hsend, hrecv, isend, irecv, lsem,
):
    g = lax.axis_index("grp")
    me = lax.axis_index("pen")
    s = lax.axis_index("gz")
    _, _, levels, rows, width = u.shape
    halves = width // LANES
    chunks = 2 * 3 * levels * halves // pens
    group_count = 2 * levels * halves
    other = 1 - g
    below, above = s > 0, s < heights - 1

    barrier = pltpu.get_barrier_semaphore()

    @pl.loop(1, pens)
    def _(i):
        pl.semaphore_signal(
            barrier, inc=1, device_id={"pen": lax.rem(me + i, pens)}, device_id_type=MESH
        )

    pl.semaphore_signal(barrier, inc=1, device_id={"grp": other}, device_id_type=MESH)

    @pl.when(below)
    def _():
        pl.semaphore_signal(barrier, inc=1, device_id={"gz": s - 1}, device_id_type=MESH)

    @pl.when(above)
    def _():
        pl.semaphore_signal(barrier, inc=1, device_id={"gz": s + 1}, device_id_type=MESH)

    wx_copy = pltpu.make_async_copy(wx_hbm.at[:, g], wx, lsem.at[0])
    wy_copy = pltpu.make_async_copy(wy_hbm, wy, lsem.at[1])
    u_copy = pltpu.make_async_copy(u, upad.at[:, :, pl.ds(1, levels)], lsem.at[2])
    u_copy.start()
    wy_copy.start()
    wx_copy.start()

    levels_near = below.astype(jnp.int32) + above.astype(jnp.int32)
    pl.semaphore_wait(barrier, pens + levels_near)

    def place(group):
        b = 1 - lax.div(group, levels * halves)
        z = lax.rem(lax.div(group, halves), levels)
        return b, z, pl.ds(pl.multiple_of(lax.rem(group, halves) * LANES, LANES), LANES)

    def unit(k, q):
        t = k * pens + q
        b, z, x = place(lax.div(t, 3))
        return b, lax.rem(t, 3), z, slice(None), x

    def band(q):
        return pl.ds(pl.multiple_of(q * rows, rows), rows)

    def pen_copy(src, dst, phase, k, i, q):
        return pltpu.make_async_remote_copy(
            src_ref=src, dst_ref=dst, send_sem=send.at[phase, k, i],
            recv_sem=recv.at[phase, k, i], device_id={"pen": q}, device_id_type=MESH,
        )

    def own_copy(src, dst, phase, k):
        return pltpu.make_async_copy(src, dst, send.at[phase, k, 0])

    def to_lines(field, lines, phase, k):
        own_copy(field.at[unit(k, me)], lines.at[k, band(me)], phase, k).start()

        @pl.loop(1, pens)
        def _(i):
            q = lax.rem(me + i, pens)
            pen_copy(field.at[unit(k, q)], lines.at[k, band(me)], phase, k, i, q).start()

    def lines_here(field, lines, phase, k):
        own_copy(field.at[unit(k, me)], lines.at[k, band(me)], phase, k).wait()

        @pl.loop(1, pens)
        def _(i):
            q = lax.rem(me + pens - i, pens)
            pen_copy(field.at[unit(k, q)], lines.at[k, band(q)], phase, k, i, q).wait_recv()

    def to_rows(lines, field, phase, k):
        own_copy(lines.at[k, band(me)], field.at[unit(k, me)], phase, k).start()

        @pl.loop(1, pens)
        def _(i):
            q = lax.rem(me + i, pens)
            pen_copy(lines.at[k, band(q)], field.at[unit(k, me)], phase, k, i, q).start()

    def rows_here(lines, field, phase, k):
        own_copy(lines.at[k, band(me)], field.at[unit(k, me)], phase, k).wait()

        @pl.loop(1, pens)
        def _(i):
            q = lax.rem(me + pens - i, pens)
            pen_copy(lines.at[k, band(q)], field.at[unit(k, q)], phase, k, i, q).wait_recv()

    def sent(src, dst, phase):
        for k in range(chunks):

            @pl.loop(1, pens)
            def _(i, k=k):
                pen_copy(src, dst, phase, k, i, lax.rem(me + i, pens)).wait_send()

    def span(lines, result, k):
        high, low = split(lines[k])
        both = dot(wy[0], jnp.concatenate([high, low], axis=1))
        result[k] = both[:, :LANES] + both[:, LANES:] + dot(wy[1], high)

    def exchange(src, dst, n):
        return pltpu.make_async_remote_copy(
            src_ref=src, dst_ref=dst, send_sem=esend.at[n], recv_sem=erecv.at[n],
            device_id={"grp": other}, device_id_type=MESH,
        )

    def stream(mine, theirs):
        for b in range(2):
            for at, field in ((b, mine(b)), (b + 2, theirs[b])):
                high, low = split(field.reshape(3 * levels * rows, width))
                hi[:, at * width : (at + 1) * width] = high
                lo[:, at * width : (at + 1) * width] = low

    def stream_out(b):
        cols = slice(b * width, (b + 1) * width)
        part = dot(hi[...], wx[0, :, cols]) + dot(hi[...], wx[1, :, cols])
        part = part + dot(lo[...], wx[0, :, cols])
        return part.reshape(3, levels, rows, width)

    def up_copy(field, n):
        return pltpu.make_async_remote_copy(
            src_ref=field.at[:, :, levels], dst_ref=field.at[:, :, 0],
            send_sem=hsend.at[n, 0], recv_sem=hrecv.at[n, 0],
            device_id={"gz": s + 1}, device_id_type=MESH,
        )

    def down_copy(field, n):
        return pltpu.make_async_remote_copy(
            src_ref=field.at[:, :, 1], dst_ref=field.at[:, :, levels + 1],
            send_sem=hsend.at[n, 1], recv_sem=hrecv.at[n, 1],
            device_id={"gz": s - 1}, device_id_type=MESH,
        )

    def send_levels(field, n):
        @pl.when(above)
        def _():
            up_copy(field, n).start()

        @pl.when(below)
        def _():
            down_copy(field, n).start()

    def levels_here(field, n):
        edge = jnp.zeros((2, 3, rows, width), F32)

        @pl.when(below)
        def _():
            down_copy(field, n).wait_send()
            up_copy(field, n).wait_recv()

        @pl.when(jnp.logical_not(below))
        def _():
            field[:, :, 0] = edge

        @pl.when(above)
        def _():
            up_copy(field, n).wait_send()
            down_copy(field, n).wait_recv()

        @pl.when(jnp.logical_not(above))
        def _():
            field[:, :, levels + 1] = edge

    def over_slabs(first, last, step):
        @pl.loop(first * (rows // SLAB), last * (rows // SLAB))
        def _(n):
            b, z, x = place(lax.div(n, rows // SLAB))
            r = pl.ds(pl.multiple_of(lax.rem(n, rows // SLAB) * SLAB, SLAB), SLAB)
            step(b, z, r, x)

    def fluxes(b, z, r, x):
        speed = [upad[b, c, z + 1, r, x] for c in range(3)]
        grad = [
            [gx[b, c, z, r, x] for c in range(3)],
            [gy[b, c, z, r, x] for c in range(3)],
            [0.5 * (upad[b, c, z + 2, r, x] - upad[b, c, z, r, x]) for c in range(3)],
        ]
        for c in range(3):
            acc[b, c, z, r, x] = -(
                speed[0] * grad[0][c] + speed[1] * grad[1][c] + speed[2] * grad[2][c]
            )
        strain = {}
        squares = 0.0
        for i in range(3):
            for j in range(i, 3):
                value = grad[i][i] if i == j else 0.5 * (grad[i][j] + grad[j][i])
                strain[i, j] = strain[j, i] = value
                squares = squares + (1.0 if i == j else 2.0) * value * value
        eddy = (2.0 * SMAGORINSKY) * jnp.sqrt(2.0 * squares)
        for c in range(3):
            fx[b, c, z, r, x] = eddy * strain[c, 0]
            fy[b, c, z, r, x] = eddy * strain[c, 1]
            fz[b, c, z + 1, r, x] = eddy * strain[c, 2]

    def add_rest(b, z, r, x):
        for c in range(3):
            rise = 0.5 * (fz[b, c, z + 2, r, x] - fz[b, c, z, r, x])
            total = acc[b, c, z, r, x] + gx[b, c, z, r, x] + rise
            acc[b, c, z, r, x] = upad[b, c, z + 1, r, x] + TIMESTEP * total

    def add_span(b, z, r, x):
        for c in range(3):
            out[b, c, z, r, x] = acc[b, c, z, r, x] + TIMESTEP * dy[b, c, z, r, x]

    def groups_ready(k):
        return (k + 1) * pens // 3

    def groups_needed(k):
        return -(-((k + 1) * pens) // 3)

    x_exchange = exchange(u, urecv, 0)
    for k in range(min(2, chunks)):
        to_lines(u, colu, 0, k)
        if k == 0:
            x_exchange.start()
    u_copy.wait()
    send_levels(upad, 0)
    wy_copy.wait()
    lines_here(u, colu, 0, 0)
    for k in range(2, chunks):
        to_lines(u, colu, 0, k)
    span(colu, coly, 0)
    to_rows(coly, gy, 1, 0)
    for k in range(1, chunks):
        lines_here(u, colu, 0, k)
        span(colu, coly, k)
        to_rows(coly, gy, 1, k)
        if k == 1:
            wx_copy.wait()
            x_exchange.wait()
            stream(lambda b: upad[b, :, 1 : levels + 1], urecv)
            for b in range(2):
                gx[b] = stream_out(b)
    levels_here(upad, 0)

    done, started = 0, 0
    for k in range(chunks):
        rows_here(coly, gy, 1, k)
        over_slabs(done, groups_ready(k), fluxes)
        done = groups_ready(k)
        while started < chunks and groups_needed(started) <= done:
            to_lines(fy, colf, 2, started)
            started += 1

    flux_exchange = exchange(fx, frecv, 1)
    flux_exchange.start()
    send_levels(fz, 1)

    columns = index.shape[1]
    third = columns // 3
    weight = jnp.zeros((1, columns), F32)
    for t in range(table.shape[0]):
        weight = weight + jnp.where(index[...] == t, table[t], 0.0)
    weight = jnp.broadcast_to(weight, (8, columns))
    cell = lax.broadcasted_iota(jnp.int32, (width, columns), 0)
    chosen = jnp.where(cell == source[...], 1.0, 0.0).astype(BF16)
    plane = lax.broadcasted_iota(jnp.int32, (columns, LANES), 0)
    slot = lax.broadcasted_iota(jnp.int32, (columns, LANES), 1)
    picks, weights = [], []
    for b in range(2):
        first = 2 * g if b == 0 else 1 - 4 * columns * g
        spread = jnp.where(
            jnp.logical_and(plane == 3 * slot + first, slot < third), 1.0, 0.0
        )
        picks.append(dot(chosen, spread.astype(BF16)).astype(BF16))
        weights.append(
            jnp.dot(weight, spread, precision=lax.Precision.HIGHEST, preferred_element_type=F32)
        )

    lines_here(fy, colf, 2, 0)
    span(colf, cold, 0)
    to_rows(cold, dy, 3, 0)
    flux_exchange.wait()
    stream(lambda b: fx[b], frecv)
    for b in range(2):
        gx[b] = stream_out(b)
    for k in range(1, chunks):
        lines_here(fy, colf, 2, k)
        span(colf, cold, k)
        to_rows(cold, dy, 3, k)
    levels_here(fz, 1)
    over_slabs(0, group_count, add_rest)

    def feed(b, parts):
        both = dot(parts[0], picks[b]) + dot(parts[1], picks[b])
        fed[b] = both.reshape(3, levels, rows, LANES)

    def blend(b, z):
        head = out[b, :, z, :, :LANES]
        out[b, :, z, :, :LANES] = head + weights[b][0:1] * (fed[b, :, z] - head)

    inflow_copy = pltpu.make_async_remote_copy(
        src_ref=out.at[1], dst_ref=inflow, send_sem=isend, recv_sem=irecv,
        device_id={"grp": other}, device_id_type=MESH,
    )
    done, half = 0, group_count // 2
    for k in range(chunks):
        rows_here(cold, dy, 3, k)
        ready = groups_ready(k)
        if done < half <= ready:
            over_slabs(done, half, add_span)
            done = half

            @pl.when(g == 1)
            def _():
                inflow_copy.start()
                inflow[...] = out[1]

            over_slabs(done, ready, add_span)
            done = ready

            @pl.when(g == 0)
            def _():
                inflow_copy.wait_recv()

            @pl.when(g == 1)
            def _():
                inflow_copy.wait_send()

            parts = split(inflow[...].reshape(3 * levels * rows, width))
            for b in range(2):
                feed(b, parts)
            for z in range(levels):
                blend(1, z)
        elif done < ready:
            over_slabs(done, ready, add_span)
            done = ready
    for z in range(levels):
        blend(0, z)
    for phase, src, dst in (
        (0, u.at[unit(0, 0)], colu.at[0, band(0)]),
        (1, coly.at[0, band(0)], gy.at[unit(0, 0)]),
        (2, fy.at[unit(0, 0)], colf.at[0, band(0)]),
        (3, cold.at[0, band(0)], dy.at[unit(0, 0)]),
    ):
        sent(src, dst, phase)


def per_device(pens, heights, velocity, source, index, table):
    _, _, levels, rows, width = velocity.shape
    line = rows * pens
    chunks = 2 * 3 * levels * (width // LANES) // pens
    wx = two_parts(stream_table(width))
    wy = two_parts(span_table(line, pens))
    flat = 3 * levels * rows
    whole = pltpu.VMEM(velocity.shape, F32)
    padded = pltpu.VMEM((2, 3, levels + 2, rows, width), F32)
    lines = pltpu.VMEM((chunks, line, LANES), F32)
    vmem = pl.BlockSpec(memory_space=pltpu.VMEM)
    dma = pltpu.SemaphoreType.DMA
    return pl.pallas_call(
        functools.partial(kernel, pens, heights),
        out_shape=pltpu.VMEM(velocity.shape, F32),
        in_specs=[
            pl.BlockSpec(memory_space=pl.ANY), vmem, vmem, pl.BlockSpec(memory_space=pltpu.SMEM),
            pl.BlockSpec(memory_space=pl.ANY), pl.BlockSpec(memory_space=pl.ANY),
        ],
        out_specs=vmem,
        scratch_shapes=[
            pltpu.VMEM((2, 4 * width, 2 * width), BF16),
            pltpu.VMEM((2, line, line), BF16),
            padded, whole, whole, whole, whole, whole, padded, whole, whole, whole,
            lines, lines, lines, lines,
            pltpu.VMEM((flat, 4 * width), BF16),
            pltpu.VMEM((flat, 4 * width), BF16),
            pltpu.VMEM(velocity.shape[1:], F32),
            pltpu.VMEM((2, 3, levels, rows, LANES), F32),
            dma((4, chunks, pens)), dma((4, chunks, pens)),
            dma((2,)), dma((2,)), dma((2, 2)), dma((2, 2)), dma, dma, dma((3,)),
        ],
        compiler_params=pltpu.CompilerParams(
            collective_id=0, has_side_effects=True, vmem_limit_bytes=56 * 1024 * 1024
        ),
    )(velocity, source.reshape(1, -1), index.reshape(1, -1), table, jnp.asarray(wx), jnp.asarray(wy))


def solution(mesh):
    placed = P("grp", None, "gz", "pen", None)
    return jax.shard_map(
        functools.partial(per_device, mesh.shape["pen"], mesh.shape["gz"]),
        mesh=mesh,
        in_specs=(placed, P(), P(), P()),
        out_specs=placed,
        check_vma=False,
    )
```
